32 devices in a mesh: seq: 4 (over y, x), blk: 8 (over z, core).
Axes of the slice: x: 2, y: 2, z: 4, core: 2. Of those that a mesh axis runs over, the one named last changes fastest.
Arguments:
- activations: bfloat16 [2, 16, 512, 4096], P(None, 'blk', 'seq'), may hold values from -120 to 120, as said below
- out_grads: bfloat16 [2, 16, 512, 4096], P(None, 'blk', 'seq'), may hold values from -120 to 120, as said below
- lengths: int32 [16], P('blk'), may hold values from 256 to 512
- input_proj: bfloat16 [2, 64, 4096], replicated, may hold values from -0.09375 to 0.09375
- output_proj: bfloat16 [2, 64, 4096], replicated, may hold values from -0.09375 to 0.09375
- stored_proj: float32 [2048, 2, 64, 64], P(('seq', 'blk')), may hold values from -6 to 6
Outputs:
- scores: float32 [16, 2048], P('blk', 'seq')
The draws below stay inside these ranges and needn't reach their ends.
Inputs may be any that keep to these rules, and one draw needn't show every extreme that they name: `activations`: finite values. `out_grads`: finite values.
All inputs are finite; a program needn't handle non-finite values.
Results may differ from the reference program's by a relative error of at most 0.0003.
Values sent between devices are 32-bit elements; how exact they have to be, the bound alone decides.
A program may use at most 64 MiB of HBM per device.

```python
import math
import jax
import jax.numpy as jnp
from jax import lax

D = 4096
R = 64
L = 2
ROLLOUTS = 16
SEQ = 512
TRAIN = 2048


def shaped_draw(key, model_width):
    k_base, k_token = jax.random.split(key, 2)
    full_shape = (L, ROLLOUTS, SEQ, model_width)
    base_draw = jnp.clip(jax.random.normal(k_base, full_shape, jnp.float32), -4.0, 4.0)
    token_scale = jnp.exp(jax.random.uniform(k_token, (L, ROLLOUTS, SEQ, 1), jnp.float32, 0.0, math.log(10.0)))
    roll_place = jnp.arange(ROLLOUTS, dtype=jnp.float32) / max(ROLLOUTS - 1, 1)
    seq_place = jnp.arange(SEQ, dtype=jnp.float32) / max(SEQ - 1, 1)
    rise_factor = jnp.exp(0.5 * math.log(3.0) * (roll_place[:, None] + seq_place[None, :]))
    return (base_draw * token_scale * rise_factor[None, :, :, None]).astype(jnp.bfloat16)


def draw_activations(key, part):
    return shaped_draw(jax.random.fold_in(key, 101), D)


def draw_out_grads(key, part):
    return shaped_draw(jax.random.fold_in(key, 202), D)


def plant(values, stream_key, low, top_value):
    dims = values.shape
    spot = [jax.random.randint(jax.random.fold_in(stream_key, axis), (), 0, dims[axis]) for axis in range(len(dims))]
    values = values.at[tuple(spot)].set(low)
    longest = dims.index(max(dims))
    spot[longest] = (spot[longest] + 1) % dims[longest]
    return values.at[tuple(spot)].set(top_value)


def block_scale(key, shape, pieces, low, largest):
    factor_of = 1.0
    for position, blocks in pieces:
        draws = jax.random.uniform(jax.random.fold_in(jax.random.fold_in(key, 6), position), (blocks,), jnp.float32, low / len(pieces), largest / len(pieces))
        factor_of = factor_of * jnp.repeat(jnp.exp(draws), shape[position] // blocks).reshape((-1,) + (1,) * (len(shape) - 1 - position))
    return factor_of


def normal_values(key, dims, spread, reach, cuts=(), kind=jnp.bfloat16):
    array = spread * jax.random.normal(key, dims, jnp.float32)
    if cuts:
        array = array * block_scale(key, dims, cuts, -0.22, 0.18)
    return jnp.clip(array, -reach, reach).astype(kind)


def setup_inputs(seed: int = 0) -> dict:
    key_list = jax.random.split(jax.random.key(seed), 7)
    activations = draw_activations(jax.random.fold_in(key_list[6], 71), 0)
    out_grads = draw_out_grads(jax.random.fold_in(key_list[6], 71), 0)
    lengths = plant(jax.random.randint(key_list[2], (ROLLOUTS,), SEQ // 2, SEQ + 1), jax.random.fold_in(key_list[2], 1), SEQ // 2, SEQ).astype(jnp.int32)
    input_proj = normal_values(key_list[3], (L, R, D), D ** -0.5, 0.09375)
    output_proj = normal_values(key_list[4], (L, R, D), D ** -0.5, 0.09375)
    stored_proj = normal_values(key_list[5], (TRAIN, L, R, R), 1.0, 6.0, ((0, 32),), jnp.float32)
    return dict(activations=activations, out_grads=out_grads, lengths=lengths, input_proj=input_proj, output_proj=output_proj, stored_proj=stored_proj)


damping = 0.1

def damped_inverse(moment, token_count):
    moment_mean = moment / token_count
    proj_rank = moment_mean.shape[-1]
    identity = jnp.eye(proj_rank, dtype=jnp.float32)
    trace_part = jnp.trace(moment_mean, axis1=1, axis2=2)
    damped = moment_mean + (damping * trace_part / proj_rank)[:, None, None] * identity
    factor_low = jnp.linalg.cholesky(damped)
    return jax.vmap(lambda lower: jax.scipy.linalg.cho_solve((lower, True), identity))(factor_low)

def reference(activations, out_grads, lengths, input_proj, output_proj, stored_proj):
    hp = lax.Precision.HIGHEST
    positions = jnp.arange(SEQ, dtype=jnp.int32)
    live_mask = (positions[None, :] < lengths[:, None]).astype(jnp.float32)
    token_count = jnp.sum(live_mask)
    moments_in = []
    moments_out = []
    grad_layers = []
    for layer in range(L):

        def one_rollout(carry, item):
            tokens_in, tokens_out, mask_row = item
            projected_in = jnp.dot(tokens_in.astype(jnp.float32), input_proj[layer].T.astype(jnp.float32), preferred_element_type=jnp.float32) * mask_row[:, None]
            projected_out = jnp.dot(tokens_out.astype(jnp.float32), output_proj[layer].T.astype(jnp.float32), preferred_element_type=jnp.float32) * mask_row[:, None]
            sum_in, sum_out = carry
            sum_in = sum_in + jnp.dot(projected_in.T, projected_in, precision=hp)
            sum_out = sum_out + jnp.dot(projected_out.T, projected_out, precision=hp)
            return ((sum_in, sum_out), jnp.dot(projected_out.T, projected_in, precision=hp))
        zeros_rr = jnp.zeros((R, R), jnp.float32)
        (sum_in, sum_out), grad_proj = lax.scan(one_rollout, (zeros_rr, zeros_rr), (activations[layer], out_grads[layer], live_mask))
        moments_in.append(sum_in)
        moments_out.append(sum_out)
        grad_layers.append(grad_proj)
    factor_in = damped_inverse(jnp.stack(moments_in), token_count)
    factor_out = damped_inverse(jnp.stack(moments_out), token_count)
    grad_stack = jnp.stack(grad_layers)
    left_done = jnp.einsum('lap,lrpq->lraq', factor_out, grad_stack, precision=hp)
    precond = jnp.einsum('lraq,lqk->lrak', left_done, factor_in, precision=hp)
    scores = jnp.einsum('lrak,tlak->rt', precond, stored_proj, precision=hp)
    return scores / math.sqrt(L * R * R)
```

```python
import functools
import math

import jax
import jax.numpy as jnp
from jax import lax
from jax.experimental import pallas as pl
from jax.experimental.pallas import tpu as pltpu
from jax.sharding import PartitionSpec as P

damping = 0.1
MESH = pl.DeviceIdType.MESH
f32, bf16 = jnp.float32, jnp.bfloat16
NT = (((1,), (1,)), ((), ()))
NN = (((1,), (0,)), ((), ()))
TN = (((0,), (0,)), ((), ()))


def mm(a, b, dims):
    return lax.dot_general(a, b, dims, preferred_element_type=f32)


def split(x):
    high = x.astype(bf16)
    return high, (x - high.astype(f32)).astype(bf16)


def invert(a_ref, cols_ref, layers, rank, width):
    rows = layers * rank
    lane = lax.broadcasted_iota(jnp.int32, (rows, width), 1)
    side_base = jnp.where(lane >= rank, rank, 0)
    sub8 = lax.broadcasted_iota(jnp.int32, (rank, width), 0)
    lane_in = lax.broadcasted_iota(jnp.int32, (1, width), 1) % rank
    group = 8

    def block(kb, _):
        k0 = pl.multiple_of(kb * group, group)
        mats = [a_ref[l * rank : (l + 1) * rank, :] for l in range(layers)]
        panels = [
            [
                jnp.take_along_axis(mats[l], side_base[:rank] + (k0 + j), axis=1)
                for j in range(group)
            ]
            for l in range(layers)
        ]
        heads = [a_ref[pl.ds(pl.multiple_of(l * rank + k0, group), group), :] for l in range(layers)]
        for l in range(layers):
            for j in range(group):
                cols_ref[j, l * rank : (l + 1) * rank, :] = panels[l][j]
        pheads = [
            [cols_ref[j, pl.ds(pl.multiple_of(l * rank + k0, group), group), :] for j in range(group)]
            for l in range(layers)
        ]
        sub_g = lax.broadcasted_iota(jnp.int32, (group, width), 0)
        for l in range(layers):
            for j in range(group):
                unit_row = jnp.where(lane_in == k0 + j, 1.0, 0.0)
                recip = 1.0 / pheads[l][j][j : j + 1, :]
                row = (heads[l][j : j + 1, :] + unit_row) * recip
                col_h = pheads[l][j] - jnp.where(sub_g == j, 1.0, 0.0)
                col = panels[l][j] - jnp.where(sub8 == k0 + j, 1.0, 0.0)
                heads[l] = heads[l] - col_h * row
                mats[l] = mats[l] - col * row
                for jj in range(j + 1, group):
                    part = pheads[l][jj][j : j + 1, :] * recip
                    pheads[l][jj] = pheads[l][jj] - col_h * part
                    panels[l][jj] = panels[l][jj] - col * part
        for l in range(layers):
            a_ref[l * rank : (l + 1) * rank, :] = mats[l]
        return 0

    lax.fori_loop(0, rank // group, block, 0)


def kernel(
    nseq, nblk, layers, roll_dev, seq_dev, rank, train_dev,
    act_hbm, grad_hbm, len_ref, pin_hbm, pout_hbm, store_hbm,
    out_ref,
    act, grad, pin, pout, store, pay_m, pay_g, rec_m, rec_g, part_m, gat_m, all_m, all_g,
    a_ref, cols_ref, t_ref, c_ref, s_hi, s_lo, snd, rec_s,
    load_sem, send_sem, sem1, sem2, sem3, sem4,
):
    width = 2 * rank
    seq_me, blk_me = lax.axis_index("seq"), lax.axis_index("blk")
    rows = rec_g.shape[1]
    rollouts = nblk * roll_dev
    hp = lax.Precision.HIGHEST

    loads = {}

    def load(name, src, dst):
        cp = pltpu.make_async_copy(src, dst, load_sem.at[len(loads)])
        cp.start()
        loads[name] = cp

    for l in range(layers):
        load(("pi", l), pin_hbm.at[l], pin.at[l])
        load(("po", l), pout_hbm.at[l], pout.at[l])
        for r in range(roll_dev):
            load(("a", l, r), act_hbm.at[l, r], act.at[l, r])
            load(("g", l, r), grad_hbm.at[l, r], grad.at[l, r])
    load("s", store_hbm, store)

    barrier = pltpu.get_barrier_semaphore()
    seq_peers = [lax.rem(seq_me + o, nseq) for o in range(1, nseq)]
    blk_peers = [lax.rem(blk_me + o, nblk) for o in range(1, nblk)]
    for s in seq_peers:
        pl.semaphore_signal(barrier, inc=1, device_id=(s, blk_me), device_id_type=MESH)
    for b in blk_peers:
        pl.semaphore_signal(barrier, inc=1, device_id=(seq_me, b), device_id_type=MESH)

    tok = lax.broadcasted_iota(jnp.int32, (seq_dev, width), 0) + seq_me * seq_dev
    live = [jnp.where(tok < len_ref[r], 1.0, 0.0) for r in range(roll_dev)]
    grams = {}
    for l in range(layers):
        loads[("pi", l)].wait()
        loads[("po", l)].wait()
        for r in range(roll_dev):
            loads[("a", l, r)].wait()
            pr_in = mm(act[l, r], pin[l], NT)
            loads[("g", l, r)].wait()
            pr_out = mm(grad[l, r], pout[l], NT)
            both = jnp.concatenate([pr_in, pr_out], axis=1) * live[r]
            grams[l, r] = lax.dot_general(both, both, TN, precision=hp, preferred_element_type=f32)
    count = sum(jnp.sum(live[r], axis=0, keepdims=True) for r in range(roll_dev))
    count = jnp.broadcast_to(count, (8, width))
    per = rank // rows if rows < rank else 1
    for l in range(layers):
        total = sum(grams[l, r] for r in range(roll_dev))
        moment = jnp.concatenate([total[:rank, :rank], total[rank:, rank:]], axis=1)
        for i in range(rank // rows):
            pay_m[l * (rank // rows) + i, :rows, :] = moment[i * rows : (i + 1) * rows]
    for r in range(roll_dev):
        g = jnp.concatenate([grams[l, r][rank:, :rank] for l in range(layers)], axis=1)
        for i in range(rank // rows):
            pay_g[r * (rank // rows) + i] = g[i * rows : (i + 1) * rows]
    for s in range(nseq):
        pay_m[s, rows:, :] = count

    pl.semaphore_wait(barrier, nseq - 1 + nblk - 1)

    sends = [0]
    started = []

    def send(src, dst, sem, dev):
        cp = pltpu.make_async_remote_copy(
            src_ref=src, dst_ref=dst, send_sem=send_sem.at[sends[0]], recv_sem=sem,
            device_id=dev, device_id_type=MESH,
        )
        sends[0] += 1
        cp.start()
        started.append(cp)
        return cp

    one_m = [send(pay_m.at[s], rec_m.at[o], sem1.at[0, o], (s, blk_me)) for o, s in enumerate(seq_peers)]
    one_g = [send(pay_g.at[s], rec_g.at[o], sem1.at[1, o], (s, blk_me)) for o, s in enumerate(seq_peers)]

    loads["s"].wait()
    quarter = rank // 4

    def prep(first):
        def one(i, _):
            for u in range(4):
                a = first + i * 4 + u
                parts = [
                    store[pl.ds(l * rank + a, train_dev, stride=layers * rank), :] for l in range(layers)
                ]
                hi, lo = split(jnp.concatenate(parts, axis=1))
                at = pl.ds(pl.multiple_of(a * width, width), width)
                s_hi[:, at] = hi
                s_lo[:, at] = lo
            return 0

        lax.fori_loop(0, quarter // 4, one, 0)

    prep(0)
    for cp in one_m:
        cp.wait_recv()
    part_m[...] = pay_m[seq_me] + sum(rec_m[o] for o in range(nseq - 1))

    two_m = [send(part_m, gat_m.at[blk_me], sem2.at[0, o], (seq_me, b)) for o, b in enumerate(blk_peers)]
    for cp in one_g:
        cp.wait_recv()
    all_g[blk_me, seq_me] = pay_g[seq_me] + sum(rec_g[o] for o in range(nseq - 1))
    mine = all_g.at[blk_me, seq_me]
    two_g = [send(mine, mine, sem2.at[1, o], (seq_me, b)) for o, b in enumerate(blk_peers)]
    gat_m[blk_me] = part_m[...]
    prep(quarter)
    for cp in two_m:
        cp.wait_recv()
    whole_m = gat_m[0]
    for b in range(1, nblk):
        whole_m = whole_m + gat_m[b]
    all_m[seq_me] = whole_m[:rows]
    token_count = whole_m[rows : rows + 1, :]

    mine_m = all_m.at[seq_me]
    three_m = [send(mine_m, mine_m, sem3.at[0, o], (s, blk_me)) for o, s in enumerate(seq_peers)]
    for cp in two_g:
        cp.wait_recv()
    mine_g = all_g.at[:, seq_me]
    three_g = [send(mine_g, mine_g, sem3.at[1, o], (s, blk_me)) for o, s in enumerate(seq_peers)]
    prep(2 * quarter)
    prep(3 * quarter)
    for cp in three_m:
        cp.wait_recv()

    moments = all_m[...].reshape(layers * rank, width)
    row_id = lax.broadcasted_iota(jnp.int32, (rank, width), 0)
    lane_id = lax.broadcasted_iota(jnp.int32, (rank, width), 1)
    on_diag = row_id == lane_id % rank
    left = lane_id[:1] < rank
    scales = []
    for l in range(layers):
        m = moments[l * rank : (l + 1) * rank]
        diag = jnp.sum(jnp.where(on_diag, m, 0.0), axis=0, keepdims=True)
        tr_in = jnp.sum(jnp.where(left, diag, 0.0), axis=1, keepdims=True)
        tr_out = jnp.sum(jnp.where(left, 0.0, diag), axis=1, keepdims=True)
        scale = rank / jnp.where(left, tr_in, tr_out)
        scales.append(scale)
        a_ref[l * rank : (l + 1) * rank, :] = m * scale + jnp.where(on_diag, damping, 0.0)
    invert(a_ref, cols_ref, layers, rank, width)
    inverses = [
        a_ref[l * rank : (l + 1) * rank, :] * (scales[l] * token_count) for l in range(layers)
    ]
    zero = jnp.zeros((rank, rank), f32)
    right = jnp.concatenate(
        [
            jnp.concatenate([inverses[l][:, :rank] if c == l else zero for c in range(layers)], axis=1)
            for l in range(layers)
        ],
        axis=0,
    )
    right_h, right_l = split(right)
    left_f = jnp.concatenate([inverses[l][:, rank:] for l in range(layers)], axis=0)
    left_h, left_l = split(left_f)

    for cp in three_g:
        cp.wait_recv()

    def apply(b, _):
        g = all_g[b].reshape(roll_dev * rank, width)
        g_h, g_l = split(g)
        t = mm(g_h, right_h, NN) + mm(g_l, right_h, NN) + mm(g_h, right_l, NN)
        for r in range(roll_dev):
            t_h, t_l = split(t[r * rank : (r + 1) * rank])
            x = mm(left_h, t_h, NN) + mm(left_l, t_h, NN) + mm(left_h, t_l, NN)
            packed = jnp.where(lane_id < rank, x[:rank], x[rank:])
            c_ref[pl.ds(pl.multiple_of((b * roll_dev + r) * rank, rank), rank), :] = packed
        return 0

    if nblk <= 8:
        for b in range(nblk):
            apply(b, 0)
    else:
        lax.fori_loop(0, nblk, apply, 0)

    c2 = jnp.concatenate([c_ref[pl.ds(a, rollouts, stride=rank), :] for a in range(rank)], axis=1)
    c_h, c_l = split(c2)
    s_h = s_hi[...]
    sc = mm(c_h, s_h, NT) + mm(c_l, s_h, NT) + mm(c_h, s_lo[...], NT)
    sc = sc * (1.0 / math.sqrt(layers * rank * rank))
    sc = jnp.concatenate([sc, sc], axis=1)
    for b in range(nblk):
        snd[b] = sc[b * roll_dev : (b + 1) * roll_dev]
    four = [send(snd.at[b], rec_s.at[blk_me], sem4.at[o], (seq_me, b)) for o, b in enumerate(blk_peers)]
    rec_s[blk_me] = snd[blk_me]
    for cp in four:
        cp.wait_recv()
    per_tile = width // train_dev
    for i in range(nblk // per_tile):
        out_ref[:, i * width : (i + 1) * width] = jnp.where(
            left, rec_s[per_tile * i], rec_s[per_tile * i + 1]
        )
    for cp in started:
        cp.wait_send()


def shards(nseq, nblk, activations, out_grads, lengths, input_proj, output_proj, stored_proj):
    layers, roll_dev, seq_dev, model_width = activations.shape
    rank = input_proj.shape[1]
    train_dev = stored_proj.shape[0]
    width = 2 * rank
    rows = layers * rank // nseq
    rollouts = nblk * roll_dev
    assert layers == 2 and roll_dev == 2 and train_dev == rank
    any_spec = pl.BlockSpec(memory_space=pl.ANY)
    n_loads = layers * 2 + layers * roll_dev * 2 + 1
    n_sends = 4 * (nseq - 1) + 3 * (nblk - 1)
    stored = stored_proj.reshape(train_dev * layers * rank, rank)
    flops = 4 * layers * roll_dev * seq_dev * model_width * rank
    return pl.pallas_call(
        functools.partial(kernel, nseq, nblk, layers, roll_dev, seq_dev, rank, train_dev),
        out_shape=jax.ShapeDtypeStruct((roll_dev, nblk * train_dev), f32),
        in_specs=[
            any_spec, any_spec, pl.BlockSpec(memory_space=pltpu.SMEM), any_spec, any_spec, any_spec,
        ],
        out_specs=pl.BlockSpec(memory_space=pltpu.VMEM),
        scratch_shapes=[
            pltpu.VMEM(activations.shape, bf16),
            pltpu.VMEM(out_grads.shape, bf16),
            pltpu.VMEM(input_proj.shape, bf16),
            pltpu.VMEM(output_proj.shape, bf16),
            pltpu.VMEM(stored.shape, f32),
            pltpu.VMEM((nseq, rows + 8, width), f32),
            pltpu.VMEM((nseq, rows, width), f32),
            pltpu.VMEM((nseq - 1, rows + 8, width), f32),
            pltpu.VMEM((nseq - 1, rows, width), f32),
            pltpu.VMEM((rows + 8, width), f32),
            pltpu.VMEM((nblk, rows + 8, width), f32),
            pltpu.VMEM((nseq, rows, width), f32),
            pltpu.VMEM((nblk, nseq, rows, width), f32),
            pltpu.VMEM((layers * rank, width), f32),
            pltpu.VMEM((8, layers * rank, width), f32),
            pltpu.VMEM((8, width), f32),
            pltpu.VMEM((rollouts * rank, width), f32),
            pltpu.VMEM((train_dev, rank * width), bf16),
            pltpu.VMEM((train_dev, rank * width), bf16),
            pltpu.VMEM((nblk, roll_dev, width), f32),
            pltpu.VMEM((nblk, roll_dev, width), f32),
            pltpu.SemaphoreType.DMA((n_loads,)),
            pltpu.SemaphoreType.DMA((n_sends,)),
            pltpu.SemaphoreType.DMA((2, nseq - 1)),
            pltpu.SemaphoreType.DMA((2, nblk - 1)),
            pltpu.SemaphoreType.DMA((2, nseq - 1)),
            pltpu.SemaphoreType.DMA((nblk - 1,)),
        ],
        compiler_params=pltpu.CompilerParams(
            collective_id=0, has_side_effects=True, vmem_limit_bytes=48 * 1024 * 1024
        ),
        cost_estimate=pl.CostEstimate(flops=flops, bytes_accessed=14 << 20, transcendentals=0),
    )(activations, out_grads, lengths, input_proj, output_proj, stored)


def solution(mesh):
    return jax.shard_map(
        functools.partial(shards, mesh.shape["seq"], mesh.shape["blk"]),
        mesh=mesh,
        in_specs=(
            P(None, "blk", "seq", None),
            P(None, "blk", "seq", None),
            P("blk"),
            P(),
            P(),
            P(("seq", "blk"), None, None, None),
        ),
        out_specs=P("blk", "seq"),
        check_vma=False,
    )
```

```python
import functools
import math

import jax
import jax.numpy as jnp
from jax import lax
from jax.experimental import pallas as pl
from jax.experimental.pallas import tpu as pltpu
from jax.sharding import PartitionSpec as P

damping = 0.1
MESH = pl.DeviceIdType.MESH
f32, bf16 = jnp.float32, jnp.bfloat16
NT = (((1,), (1,)), ((), ()))
NN = (((1,), (0,)), ((), ()))
TN = (((0,), (0,)), ((), ()))


def mm(a, b, dims):
    return lax.dot_general(a, b, dims, preferred_element_type=f32)


def split(x):
    high = x.astype(bf16)
    return high, (x - high.astype(f32)).astype(bf16)


def invert(a_ref, cols_ref, layers, rank, width):
    rows = layers * rank
    lane = lax.broadcasted_iota(jnp.int32, (rows, width), 1)
    side_base = jnp.where(lane >= rank, rank, 0)
    sub8 = lax.broadcasted_iota(jnp.int32, (rank, width), 0)
    lane_in = lax.broadcasted_iota(jnp.int32, (1, width), 1) % rank
    group = 8

    def block(kb, _):
        k0 = pl.multiple_of(kb * group, group)
        mats = [a_ref[l * rank : (l + 1) * rank, :] for l in range(layers)]
        panels = [
            [
                jnp.take_along_axis(mats[l], side_base[:rank] + (k0 + j), axis=1)
                for j in range(group)
            ]
            for l in range(layers)
        ]
        heads = [a_ref[pl.ds(pl.multiple_of(l * rank + k0, group), group), :] for l in range(layers)]
        for l in range(layers):
            for j in range(group):
                cols_ref[j, l * rank : (l + 1) * rank, :] = panels[l][j]
        pheads = [
            [cols_ref[j, pl.ds(pl.multiple_of(l * rank + k0, group), group), :] for j in range(group)]
            for l in range(layers)
        ]
        sub_g = lax.broadcasted_iota(jnp.int32, (group, width), 0)
        for l in range(layers):
            for j in range(group):
                unit_row = jnp.where(lane_in == k0 + j, 1.0, 0.0)
                recip = 1.0 / pheads[l][j][j : j + 1, :]
                row = (heads[l][j : j + 1, :] + unit_row) * recip
                col_h = pheads[l][j] - jnp.where(sub_g == j, 1.0, 0.0)
                col = panels[l][j] - jnp.where(sub8 == k0 + j, 1.0, 0.0)
                heads[l] = heads[l] - col_h * row
                mats[l] = mats[l] - col * row
                for jj in range(j + 1, group):
                    part = pheads[l][jj][j : j + 1, :] * recip
                    pheads[l][jj] = pheads[l][jj] - col_h * part
                    panels[l][jj] = panels[l][jj] - col * part
        for l in range(layers):
            a_ref[l * rank : (l + 1) * rank, :] = mats[l]
        return 0

    lax.fori_loop(0, rank // group, block, 0)


def kernel(
    nseq, nblk, layers, roll_dev, seq_dev, rank, train_dev,
    act_hbm, grad_hbm, len_ref, pin_hbm, pout_hbm, store_hbm,
    out_ref,
    act, grad, pin, pout, store, pay_m, pay_g, rec_m, rec_g, part_m, gat_m, all_m, all_g,
    a_ref, cols_ref, t_ref, c_ref, s_hi, s_lo, snd, rec_s,
    load_sem, send_sem, sem1, sem2, sem3, sem4,
):
    width = 2 * rank
    seq_me, blk_me = lax.axis_index("seq"), lax.axis_index("blk")
    rows = rec_g.shape[1]
    nz, ng = nblk // 2, 2 * nseq
    mrows = all_m.shape[1]
    core, z_me = lax.rem(blk_me, 2), lax.div(blk_me, 2)
    group_me = seq_me * 2 + core
    rollouts = nblk * roll_dev
    hp = lax.Precision.HIGHEST

    loads = {}

    def load(name, src, dst):
        cp = pltpu.make_async_copy(src, dst, load_sem.at[len(loads)])
        cp.start()
        loads[name] = cp

    for l in range(layers):
        load(("pi", l), pin_hbm.at[l], pin.at[l])
        load(("po", l), pout_hbm.at[l], pout.at[l])
        for r in range(roll_dev):
            load(("a", l, r), act_hbm.at[l, r], act.at[l, r])
            load(("g", l, r), grad_hbm.at[l, r], grad.at[l, r])
    load("s", store_hbm, store)

    barrier = pltpu.get_barrier_semaphore()
    seq_peers = [lax.rem(seq_me + o, nseq) for o in range(1, nseq)]
    shares = [lax.rem(group_me + o, ng) for o in range(1, ng)]
    group = [(lax.div(g, 2), z_me * 2 + lax.rem(g, 2)) for g in shares]
    line = [(seq_me, lax.rem(z_me + o, nz) * 2 + core) for o in range(1, nz)]
    owners = [
        lax.rem(z_me + o, nz) * 2 + lax.rem(core + c, 2) for o in range(nz) for c in range(2) if o or c
    ]
    greet = group + [(seq_me, b) for b in owners[1:]]
    for peer in greet:
        pl.semaphore_signal(barrier, inc=1, device_id=peer, device_id_type=MESH)

    tok = lax.broadcasted_iota(jnp.int32, (seq_dev, width), 0) + seq_me * seq_dev
    live = [jnp.where(tok < len_ref[r], 1.0, 0.0) for r in range(roll_dev)]
    grams = {}
    for l in range(layers):
        loads[("pi", l)].wait()
        loads[("po", l)].wait()
        for r in range(roll_dev):
            loads[("a", l, r)].wait()
            pr_in = mm(act[l, r], pin[l], NT)
            loads[("g", l, r)].wait()
            pr_out = mm(grad[l, r], pout[l], NT)
            both = jnp.concatenate([pr_in, pr_out], axis=1) * live[r]
            grams[l, r] = lax.dot_general(both, both, TN, precision=hp, preferred_element_type=f32)
    count = sum(jnp.sum(live[r], axis=0, keepdims=True) for r in range(roll_dev))
    count = jnp.broadcast_to(count, (8, width))
    for l in range(layers):
        total = sum(grams[l, r] for r in range(roll_dev))
        moment = jnp.concatenate([total[:rank, :rank], total[rank:, rank:]], axis=1)
        for i in range(rank // mrows):
            pay_m[l * (rank // mrows) + i, :mrows, :] = moment[i * mrows : (i + 1) * mrows]
    for r in range(roll_dev):
        g = jnp.concatenate([grams[l, r][rank:, :rank] for l in range(layers)], axis=1)
        for i in range(rank // rows):
            pay_g[r * (rank // rows) + i] = g[i * rows : (i + 1) * rows]
    for g in range(ng):
        pay_m[g, mrows:, :] = count

    pl.semaphore_wait(barrier, len(greet))

    sends = [0]
    started = []

    def send(src, dst, sem, dev):
        cp = pltpu.make_async_remote_copy(
            src_ref=src, dst_ref=dst, send_sem=send_sem.at[sends[0]], recv_sem=sem,
            device_id=dev, device_id_type=MESH,
        )
        sends[0] += 1
        cp.start()
        started.append(cp)
        return cp

    one_m = [send(pay_m.at[g], rec_m.at[o], sem1.at[0, o], group[o]) for o, g in enumerate(shares)]
    one_g = [send(pay_g.at[s], rec_g.at[o], sem1.at[1, o], (s, blk_me)) for o, s in enumerate(seq_peers)]

    loads["s"].wait()
    quarter = rank // 4

    def prep(first):
        def one(i, _):
            for u in range(4):
                a = first + i * 4 + u
                parts = [
                    store[pl.ds(l * rank + a, train_dev, stride=layers * rank), :] for l in range(layers)
                ]
                hi, lo = split(jnp.concatenate(parts, axis=1))
                at = pl.ds(pl.multiple_of(a * width, width), width)
                s_hi[:, at] = hi
                s_lo[:, at] = lo
            return 0

        lax.fori_loop(0, quarter // 4, one, 0)

    prep(0)
    for cp in one_m:
        cp.wait_recv()
    part_m[...] = pay_m[group_me] + sum(rec_m[o] for o in range(ng - 1))

    two_m = [send(part_m, gat_m.at[z_me], sem2.at[0, o], peer) for o, peer in enumerate(line)]
    for cp in one_g:
        cp.wait_recv()
    all_g[z_me, core, seq_me] = pay_g[seq_me] + sum(rec_g[o] for o in range(nseq - 1))
    mine = all_g.at[z_me, core, seq_me]
    two_g = [send(mine, mine, sem2.at[1, o], peer) for o, peer in enumerate(line)]
    gat_m[z_me] = part_m[...]
    prep(quarter)
    for cp in two_m:
        cp.wait_recv()
    whole_m = gat_m[0]
    for z in range(1, nz):
        whole_m = whole_m + gat_m[z]
    all_m[group_me] = whole_m[:mrows]
    token_count = whole_m[mrows : mrows + 1, :]

    mine_m = all_m.at[group_me]
    three_m = [send(mine_m, mine_m, sem3.at[0, o], peer) for o, peer in enumerate(group)]
    for cp in two_g:
        cp.wait_recv()
    mine_g = all_g.at[:, core, seq_me]
    three_g = [send(mine_g, mine_g, sem3.at[1, o], peer) for o, peer in enumerate(group)]
    prep(2 * quarter)
    prep(3 * quarter)
    for cp in three_m:
        cp.wait_recv()

    moments = all_m[...].reshape(layers * rank, width)
    row_id = lax.broadcasted_iota(jnp.int32, (rank, width), 0)
    lane_id = lax.broadcasted_iota(jnp.int32, (rank, width), 1)
    on_diag = row_id == lane_id % rank
    left = lane_id[:1] < rank
    scales = []
    for l in range(layers):
        m = moments[l * rank : (l + 1) * rank]
        diag = jnp.sum(jnp.where(on_diag, m, 0.0), axis=0, keepdims=True)
        tr_in = jnp.sum(jnp.where(left, diag, 0.0), axis=1, keepdims=True)
        tr_out = jnp.sum(jnp.where(left, 0.0, diag), axis=1, keepdims=True)
        scale = rank / jnp.where(left, tr_in, tr_out)
        scales.append(scale)
        a_ref[l * rank : (l + 1) * rank, :] = m * scale + jnp.where(on_diag, damping, 0.0)
    invert(a_ref, cols_ref, layers, rank, width)
    inverses = [
        a_ref[l * rank : (l + 1) * rank, :] * (scales[l] * token_count) for l in range(layers)
    ]
    zero = jnp.zeros((rank, rank), f32)
    right = jnp.concatenate(
        [
            jnp.concatenate([inverses[l][:, :rank] if c == l else zero for c in range(layers)], axis=1)
            for l in range(layers)
        ],
        axis=0,
    )
    right_h, right_l = split(right)
    left_f = jnp.concatenate([inverses[l][:, rank:] for l in range(layers)], axis=0)
    left_h, left_l = split(left_f)

    for cp in three_g:
        cp.wait_recv()

    def apply(b, _):
        g = all_g[b // 2, b % 2].reshape(roll_dev * rank, width)
        g_h, g_l = split(g)
        t = mm(g_h, right_h, NN) + mm(g_l, right_h, NN) + mm(g_h, right_l, NN)
        for r in range(roll_dev):
            t_h, t_l = split(t[r * rank : (r + 1) * rank])
            x = mm(left_h, t_h, NN) + mm(left_l, t_h, NN) + mm(left_h, t_l, NN)
            packed = jnp.where(lane_id < rank, x[:rank], x[rank:])
            c_ref[pl.ds(pl.multiple_of((b * roll_dev + r) * rank, rank), rank), :] = packed
        return 0

    if nblk <= 8:
        for b in range(nblk):
            apply(b, 0)
    else:
        lax.fori_loop(0, nblk, apply, 0)

    c2 = jnp.concatenate([c_ref[pl.ds(a, rollouts, stride=rank), :] for a in range(rank)], axis=1)
    c_h, c_l = split(c2)
    s_h = s_hi[...]
    sc = mm(c_h, s_h, NT) + mm(c_l, s_h, NT) + mm(c_h, s_lo[...], NT)
    sc = sc * (1.0 / math.sqrt(layers * rank * rank))
    sc = jnp.concatenate([sc, sc], axis=1)
    for b in range(nblk):
        snd[b] = sc[b * roll_dev : (b + 1) * roll_dev]
    four = [send(snd.at[b], rec_s.at[blk_me], sem4.at[o], (seq_me, b)) for o, b in enumerate(owners)]
    rec_s[blk_me] = snd[blk_me]
    for cp in four:
        cp.wait_recv()
    per_tile = width // train_dev
    for i in range(nblk // per_tile):
        out_ref[:, i * width : (i + 1) * width] = jnp.where(
            left, rec_s[per_tile * i], rec_s[per_tile * i + 1]
        )
    for cp in started:
        cp.wait_send()


def shards(nseq, nblk, activations, out_grads, lengths, input_proj, output_proj, stored_proj):
    layers, roll_dev, seq_dev, model_width = activations.shape
    rank = input_proj.shape[1]
    train_dev = stored_proj.shape[0]
    width = 2 * rank
    rows = layers * rank // nseq
    rollouts = nblk * roll_dev
    assert layers == 2 and roll_dev == 2 and train_dev == rank
    any_spec = pl.BlockSpec(memory_space=pl.ANY)
    n_loads = layers * 2 + layers * roll_dev * 2 + 1
    ng, nz = 2 * nseq, nblk // 2
    mrows = layers * rank // ng
    n_sends = 3 * (ng - 1) + (nseq - 1) + 2 * (nz - 1) + nblk - 1
    stored = stored_proj.reshape(train_dev * layers * rank, rank)
    flops = 4 * layers * roll_dev * seq_dev * model_width * rank
    return pl.pallas_call(
        functools.partial(kernel, nseq, nblk, layers, roll_dev, seq_dev, rank, train_dev),
        out_shape=jax.ShapeDtypeStruct((roll_dev, nblk * train_dev), f32),
        in_specs=[
            any_spec, any_spec, pl.BlockSpec(memory_space=pltpu.SMEM), any_spec, any_spec, any_spec,
        ],
        out_specs=pl.BlockSpec(memory_space=pltpu.VMEM),
        scratch_shapes=[
            pltpu.VMEM(activations.shape, bf16),
            pltpu.VMEM(out_grads.shape, bf16),
            pltpu.VMEM(input_proj.shape, bf16),
            pltpu.VMEM(output_proj.shape, bf16),
            pltpu.VMEM(stored.shape, f32),
            pltpu.VMEM((ng, mrows + 8, width), f32),
            pltpu.VMEM((nseq, rows, width), f32),
            pltpu.VMEM((ng - 1, mrows + 8, width), f32),
            pltpu.VMEM((nseq - 1, rows, width), f32),
            pltpu.VMEM((mrows + 8, width), f32),
            pltpu.VMEM((nz, mrows + 8, width), f32),
            pltpu.VMEM((ng, mrows, width), f32),
            pltpu.VMEM((nz, 2, nseq, rows, width), f32),
            pltpu.VMEM((layers * rank, width), f32),
            pltpu.VMEM((8, layers * rank, width), f32),
            pltpu.VMEM((8, width), f32),
            pltpu.VMEM((rollouts * rank, width), f32),
            pltpu.VMEM((train_dev, rank * width), bf16),
            pltpu.VMEM((train_dev, rank * width), bf16),
            pltpu.VMEM((nblk, roll_dev, width), f32),
            pltpu.VMEM((nblk, roll_dev, width), f32),
            pltpu.SemaphoreType.DMA((n_loads,)),
            pltpu.SemaphoreType.DMA((n_sends,)),
            pltpu.SemaphoreType.DMA((2, ng - 1)),
            pltpu.SemaphoreType.DMA((2, nz - 1)),
            pltpu.SemaphoreType.DMA((2, ng - 1)),
            pltpu.SemaphoreType.DMA((nblk - 1,)),
        ],
        compiler_params=pltpu.CompilerParams(
            collective_id=0, has_side_effects=True, vmem_limit_bytes=60 * 1024 * 1024
        ),
        cost_estimate=pl.CostEstimate(flops=flops, bytes_accessed=14 << 20, transcendentals=0),
    )(activations, out_grads, lengths, input_proj, output_proj, stored)


def solution(mesh):
    return jax.shard_map(
        functools.partial(shards, mesh.shape["seq"], mesh.shape["blk"]),
        mesh=mesh,
        in_specs=(
            P(None, "blk", "seq", None),
            P(None, "blk", "seq", None),
            P("blk"),
            P(),
            P(),
            P(("seq", "blk"), None, None, None),
        ),
        out_specs=P("blk", "seq"),
        check_vma=False,
    )
```

```python
import functools
import math

import jax
import jax.numpy as jnp
from jax import lax
from jax.experimental import pallas as pl
from jax.experimental.pallas import tpu as pltpu
from jax.sharding import PartitionSpec as P

damping = 0.1
MESH = pl.DeviceIdType.MESH
f32, bf16 = jnp.float32, jnp.bfloat16
NT = (((1,), (1,)), ((), ()))
NN = (((1,), (0,)), ((), ()))
TN = (((0,), (0,)), ((), ()))


def mm(a, b, dims):
    return lax.dot_general(a, b, dims, preferred_element_type=f32)


def split(x):
    high = x.astype(bf16)
    return high, (x - high.astype(f32)).astype(bf16)


def invert(a_ref, cols_ref, layers, rank, width):
    rows = layers * rank
    lane = lax.broadcasted_iota(jnp.int32, (rows, width), 1)
    side_base = jnp.where(lane >= rank, rank, 0)
    sub8 = lax.broadcasted_iota(jnp.int32, (rank, width), 0)
    lane_in = lax.broadcasted_iota(jnp.int32, (1, width), 1) % rank
    group = 8

    def block(kb, _):
        k0 = pl.multiple_of(kb * group, group)
        mats = [a_ref[l * rank : (l + 1) * rank, :] for l in range(layers)]
        panels = [
            [
                jnp.take_along_axis(mats[l], side_base[:rank] + (k0 + j), axis=1)
                for j in range(group)
            ]
            for l in range(layers)
        ]
        heads = [a_ref[pl.ds(pl.multiple_of(l * rank + k0, group), group), :] for l in range(layers)]
        for l in range(layers):
            for j in range(group):
                cols_ref[j, l * rank : (l + 1) * rank, :] = panels[l][j]
        pheads = [
            [cols_ref[j, pl.ds(pl.multiple_of(l * rank + k0, group), group), :] for j in range(group)]
            for l in range(layers)
        ]
        sub_g = lax.broadcasted_iota(jnp.int32, (group, width), 0)
        for l in range(layers):
            for j in range(group):
                unit_row = jnp.where(lane_in == k0 + j, 1.0, 0.0)
                recip = 1.0 / pheads[l][j][j : j + 1, :]
                row = (heads[l][j : j + 1, :] + unit_row) * recip
                col_h = pheads[l][j] - jnp.where(sub_g == j, 1.0, 0.0)
                col = panels[l][j] - jnp.where(sub8 == k0 + j, 1.0, 0.0)
                heads[l] = heads[l] - col_h * row
                mats[l] = mats[l] - col * row
                for jj in range(j + 1, group):
                    part = pheads[l][jj][j : j + 1, :] * recip
                    pheads[l][jj] = pheads[l][jj] - col_h * part
                    panels[l][jj] = panels[l][jj] - col * part
        for l in range(layers):
            a_ref[l * rank : (l + 1) * rank, :] = mats[l]
        return 0

    lax.fori_loop(0, rank // group, block, 0)


def kernel(
    nseq, nblk, layers, roll_dev, seq_dev, rank, train_dev,
    act_hbm, grad_hbm, len_ref, pin_hbm, pout_hbm, store_hbm,
    out_ref,
    act, grad, pin, pout, store, pay_m, pay_g, rec_m, rec_g, part_m, gat_m, all_m, all_g,
    a_ref, cols_ref, t_ref, c_ref, s_hi, s_lo, snd, rec_s,
    load_sem, send_sem, sem1, sem2, sem3, sem4,
):
    width = 2 * rank
    seq_me, blk_me = lax.axis_index("seq"), lax.axis_index("blk")
    rows = rec_g.shape[1]
    nz, ng = nblk // 2, 2 * nseq
    mrows = all_m.shape[1]
    core, z_me = lax.rem(blk_me, 2), lax.div(blk_me, 2)
    group_me = seq_me * 2 + core
    rollouts = nblk * roll_dev
    hp = lax.Precision.HIGHEST

    loads = {}

    def load(name, src, dst):
        cp = pltpu.make_async_copy(src, dst, load_sem.at[len(loads)])
        cp.start()
        loads[name] = cp

    for l in range(layers):
        load(("pi", l), pin_hbm.at[l], pin.at[l])
        for r in range(roll_dev):
            load(("a", l, r), act_hbm.at[l, r], act.at[l, r])
        load(("po", l), pout_hbm.at[l], pout.at[l])
        for r in range(roll_dev):
            load(("g", l, r), grad_hbm.at[l, r], grad.at[l, r])
    load("s", store_hbm, store)

    barrier = pltpu.get_barrier_semaphore()
    seq_peers = [lax.rem(seq_me + o, nseq) for o in range(1, nseq)]
    shares = [lax.rem(group_me + o, ng) for o in range(1, ng)]
    group = [(lax.div(g, 2), z_me * 2 + lax.rem(g, 2)) for g in shares]
    line = [(seq_me, lax.rem(z_me + o, nz) * 2 + core) for o in range(1, nz)]
    owners = [
        lax.rem(z_me + o, nz) * 2 + lax.rem(core + c, 2) for o in range(nz) for c in range(2) if o or c
    ]
    greet = group + [(seq_me, b) for b in owners[1:]]
    for peer in greet:
        pl.semaphore_signal(barrier, inc=1, device_id=peer, device_id_type=MESH)

    tok = lax.broadcasted_iota(jnp.int32, (seq_dev, width), 0) + seq_me * seq_dev
    live = [jnp.where(tok < len_ref[r], 1.0, 0.0) for r in range(roll_dev)]
    grams = {}
    for l in range(layers):
        loads[("pi", l)].wait()
        model_width = act.shape[3]
        for r in range(roll_dev):
            loads[("a", l, r)].wait()
        pr_in = mm(act[l].reshape(roll_dev * seq_dev, model_width), pin[l], NT)
        loads[("po", l)].wait()
        for r in range(roll_dev):
            loads[("g", l, r)].wait()
        pr_out = mm(grad[l].reshape(roll_dev * seq_dev, model_width), pout[l], NT)
        pair = jnp.concatenate([pr_in, pr_out], axis=1)
        for r in range(roll_dev):
            both = pair[r * seq_dev : (r + 1) * seq_dev] * live[r]
            grams[l, r] = lax.dot_general(both, both, TN, precision=hp, preferred_element_type=f32)
    count = sum(jnp.sum(live[r], axis=0, keepdims=True) for r in range(roll_dev))
    count = jnp.broadcast_to(count, (8, width))
    for l in range(layers):
        total = sum(grams[l, r] for r in range(roll_dev))
        moment = jnp.concatenate([total[:rank, :rank], total[rank:, rank:]], axis=1)
        for i in range(rank // mrows):
            pay_m[l * (rank // mrows) + i, :mrows, :] = moment[i * mrows : (i + 1) * mrows]
    for r in range(roll_dev):
        g = jnp.concatenate([grams[l, r][rank:, :rank] for l in range(layers)], axis=1)
        for i in range(rank // rows):
            pay_g[r * (rank // rows) + i] = g[i * rows : (i + 1) * rows]
    for g in range(ng):
        pay_m[g, mrows:, :] = count

    pl.semaphore_wait(barrier, len(greet))

    sends = [0]
    started = []

    def send(src, dst, sem, dev):
        cp = pltpu.make_async_remote_copy(
            src_ref=src, dst_ref=dst, send_sem=send_sem.at[sends[0]], recv_sem=sem,
            device_id=dev, device_id_type=MESH,
        )
        sends[0] += 1
        cp.start()
        started.append(cp)
        return cp

    one_m = [send(pay_m.at[g], rec_m.at[o], sem1.at[0, o], group[o]) for o, g in enumerate(shares)]
    one_g = [send(pay_g.at[s], rec_g.at[o], sem1.at[1, o], (s, blk_me)) for o, s in enumerate(seq_peers)]

    loads["s"].wait()
    quarter = rank // 4

    def prep(first):
        def one(i, _):
            for u in range(4):
                a = first + i * 4 + u
                parts = [
                    store[pl.ds(l * rank + a, train_dev, stride=layers * rank), :] for l in range(layers)
                ]
                hi, lo = split(jnp.concatenate(parts, axis=1))
                at = pl.ds(pl.multiple_of(a * width, width), width)
                s_hi[:, at] = hi
                s_lo[:, at] = lo
            return 0

        lax.fori_loop(0, quarter // 4, one, 0)

    prep(0)
    for cp in one_m:
        cp.wait_recv()
    part_m[...] = pay_m[group_me] + sum(rec_m[o] for o in range(ng - 1))

    two_m = [send(part_m, gat_m.at[z_me], sem2.at[0, o], peer) for o, peer in enumerate(line)]
    for cp in one_g:
        cp.wait_recv()
    all_g[z_me, core, seq_me] = pay_g[seq_me] + sum(rec_g[o] for o in range(nseq - 1))
    mine = all_g.at[z_me, core, seq_me]
    two_g = [send(mine, mine, sem2.at[1, o], peer) for o, peer in enumerate(line)]
    gat_m[z_me] = part_m[...]
    prep(quarter)
    for cp in two_m:
        cp.wait_recv()
    whole_m = gat_m[0]
    for z in range(1, nz):
        whole_m = whole_m + gat_m[z]
    all_m[group_me] = whole_m[:mrows]
    token_count = whole_m[mrows : mrows + 1, :]

    mine_m = all_m.at[group_me]
    three_m = [send(mine_m, mine_m, sem3.at[0, o], peer) for o, peer in enumerate(group)]
    for cp in two_g:
        cp.wait_recv()
    mine_g = all_g.at[:, core, seq_me]
    three_g = [send(mine_g, mine_g, sem3.at[1, o], peer) for o, peer in enumerate(group)]
    prep(2 * quarter)
    prep(3 * quarter)
    for cp in three_m:
        cp.wait_recv()

    moments = all_m[...].reshape(layers * rank, width)
    row_id = lax.broadcasted_iota(jnp.int32, (rank, width), 0)
    lane_id = lax.broadcasted_iota(jnp.int32, (rank, width), 1)
    on_diag = row_id == lane_id % rank
    left = lane_id[:1] < rank
    scales = []
    for l in range(layers):
        m = moments[l * rank : (l + 1) * rank]
        diag = jnp.sum(jnp.where(on_diag, m, 0.0), axis=0, keepdims=True)
        tr_in = jnp.sum(jnp.where(left, diag, 0.0), axis=1, keepdims=True)
        tr_out = jnp.sum(jnp.where(left, 0.0, diag), axis=1, keepdims=True)
        scale = rank / jnp.where(left, tr_in, tr_out)
        scales.append(scale)
        a_ref[l * rank : (l + 1) * rank, :] = m * scale + jnp.where(on_diag, damping, 0.0)
    invert(a_ref, cols_ref, layers, rank, width)
    inverses = [
        a_ref[l * rank : (l + 1) * rank, :] * (scales[l] * token_count) for l in range(layers)
    ]
    zero = jnp.zeros((rank, rank), f32)
    right = jnp.concatenate(
        [
            jnp.concatenate([inverses[l][:, :rank] if c == l else zero for c in range(layers)], axis=1)
            for l in range(layers)
        ],
        axis=0,
    )
    right_h, right_l = split(right)
    left_f = jnp.concatenate([inverses[l][:, rank:] for l in range(layers)], axis=0)
    left_h, left_l = split(left_f)

    for cp in three_g:
        cp.wait_recv()

    def apply(b, _):
        g = all_g[b // 2, b % 2].reshape(roll_dev * rank, width)
        g_h, g_l = split(g)
        t = mm(g_h, right_h, NN) + mm(g_l, right_h, NN) + mm(g_h, right_l, NN)
        for r in range(roll_dev):
            t_h, t_l = split(t[r * rank : (r + 1) * rank])
            x = mm(left_h, t_h, NN) + mm(left_l, t_h, NN) + mm(left_h, t_l, NN)
            packed = jnp.where(lane_id < rank, x[:rank], x[rank:])
            c_ref[pl.ds(pl.multiple_of((b * roll_dev + r) * rank, rank), rank), :] = packed
        return 0

    if nblk <= 8:
        for b in range(nblk):
            apply(b, 0)
    else:
        lax.fori_loop(0, nblk, apply, 0)

    c2 = jnp.concatenate([c_ref[pl.ds(a, rollouts, stride=rank), :] for a in range(rank)], axis=1)
    c_h, c_l = split(c2)
    s_h = s_hi[...]
    sc = mm(c_h, s_h, NT) + mm(c_l, s_h, NT) + mm(c_h, s_lo[...], NT)
    sc = sc * (1.0 / math.sqrt(layers * rank * rank))
    sc = jnp.concatenate([sc, sc], axis=1)
    for b in range(nblk):
        snd[b] = sc[b * roll_dev : (b + 1) * roll_dev]
    four = [send(snd.at[b], rec_s.at[blk_me], sem4.at[o], (seq_me, b)) for o, b in enumerate(owners)]
    rec_s[blk_me] = snd[blk_me]
    for cp in four:
        cp.wait_recv()
    per_tile = width // train_dev
    for i in range(nblk // per_tile):
        out_ref[:, i * width : (i + 1) * width] = jnp.where(
            left, rec_s[per_tile * i], rec_s[per_tile * i + 1]
        )
    for cp in started:
        cp.wait_send()


def shards(nseq, nblk, activations, out_grads, lengths, input_proj, output_proj, stored_proj):
    layers, roll_dev, seq_dev, model_width = activations.shape
    rank = input_proj.shape[1]
    train_dev = stored_proj.shape[0]
    width = 2 * rank
    rows = layers * rank // nseq
    rollouts = nblk * roll_dev
    assert layers == 2 and roll_dev == 2 and train_dev == rank
    any_spec = pl.BlockSpec(memory_space=pl.ANY)
    n_loads = layers * 2 + layers * roll_dev * 2 + 1
    ng, nz = 2 * nseq, nblk // 2
    mrows = layers * rank // ng
    n_sends = 3 * (ng - 1) + (nseq - 1) + 2 * (nz - 1) + nblk - 1
    stored = stored_proj.reshape(train_dev * layers * rank, rank)
    flops = 4 * layers * roll_dev * seq_dev * model_width * rank
    return pl.pallas_call(
        functools.partial(kernel, nseq, nblk, layers, roll_dev, seq_dev, rank, train_dev),
        out_shape=jax.ShapeDtypeStruct((roll_dev, nblk * train_dev), f32),
        in_specs=[
            any_spec, any_spec, pl.BlockSpec(memory_space=pltpu.SMEM), any_spec, any_spec, any_spec,
        ],
        out_specs=pl.BlockSpec(memory_space=pltpu.VMEM),
        scratch_shapes=[
            pltpu.VMEM(activations.shape, bf16),
            pltpu.VMEM(out_grads.shape, bf16),
            pltpu.VMEM(input_proj.shape, bf16),
            pltpu.VMEM(output_proj.shape, bf16),
            pltpu.VMEM(stored.shape, f32),
            pltpu.VMEM((ng, mrows + 8, width), f32),
            pltpu.VMEM((nseq, rows, width), f32),
            pltpu.VMEM((ng - 1, mrows + 8, width), f32),
            pltpu.VMEM((nseq - 1, rows, width), f32),
            pltpu.VMEM((mrows + 8, width), f32),
            pltpu.VMEM((nz, mrows + 8, width), f32),
            pltpu.VMEM((ng, mrows, width), f32),
            pltpu.VMEM((nz, 2, nseq, rows, width), f32),
            pltpu.VMEM((layers * rank, width), f32),
            pltpu.VMEM((8, layers * rank, width), f32),
            pltpu.VMEM((8, width), f32),
            pltpu.VMEM((rollouts * rank, width), f32),
            pltpu.VMEM((train_dev, rank * width), bf16),
            pltpu.VMEM((train_dev, rank * width), bf16),
            pltpu.VMEM((nblk, roll_dev, width), f32),
            pltpu.VMEM((nblk, roll_dev, width), f32),
            pltpu.SemaphoreType.DMA((n_loads,)),
            pltpu.SemaphoreType.DMA((n_sends,)),
            pltpu.SemaphoreType.DMA((2, ng - 1)),
            pltpu.SemaphoreType.DMA((2, nz - 1)),
            pltpu.SemaphoreType.DMA((2, ng - 1)),
            pltpu.SemaphoreType.DMA((nblk - 1,)),
        ],
        compiler_params=pltpu.CompilerParams(
            collective_id=0, has_side_effects=True, vmem_limit_bytes=60 * 1024 * 1024
        ),
        cost_estimate=pl.CostEstimate(flops=flops, bytes_accessed=14 << 20, transcendentals=0),
    )(activations, out_grads, lengths, input_proj, output_proj, stored)


def solution(mesh):
    return jax.shard_map(
        functools.partial(shards, mesh.shape["seq"], mesh.shape["blk"]),
        mesh=mesh,
        in_specs=(
            P(None, "blk", "seq", None),
            P(None, "blk", "seq", None),
            P("blk"),
            P(),
            P(),
            P(("seq", "blk"), None, None, None),
        ),
        out_specs=P("blk", "seq"),
        check_vma=False,
    )
```
